512 devices in a mesh: freq: 32 (over x, z_lo, core), tile: 16 (over y, z_hi).
Axes of the slice: x: 4, y: 8, z: 8 (z_hi: 2, z_lo: 4; z = z_hi * 4 + z_lo), core: 2. Of those that a mesh axis runs over, the one named last changes fastest.
Arguments:
- source_field: float32 [2, 32, 256, 1024], P(None, 'freq', 'tile'), may hold values from -6 to 6
- receiver_field: float32 [2, 32, 256, 1024], P(None, 'freq', 'tile'), may hold values from -6 to 6
- velocity_store: float32 [32, 256, 1024], P('freq', 'tile'), may hold values from 0.5 to 1
- slice_owner: int32 [4], replicated, may hold values from 0 to 31, as said below
- region_map: int32 [256, 1024], P('tile', 'freq'), may hold values from 0 to 3, as said below
Outputs:
- wavefields: float32 [2, 2, 32, 256, 1024], P(None, None, 'freq', 'tile')
- smoothed_image: float32 [4, 256, 1024], P(None, 'tile', 'freq')
The draws below stay inside these ranges and needn't reach their ends.
Inputs may be any that keep to these rules, and one draw needn't show every extreme that they name: `slice_owner`: the 4 entries are distinct stored-slice indices; slices 0 and 31 are always among them. `region_map`: labels along the second lateral dimension change at scattered cells.
All inputs are finite; a program needn't handle non-finite values.
Results may differ from the reference program's by a relative error of at most 0.000023.
Values sent between devices are 32-bit elements; how exact they have to be, the bound alone decides.
A program may use at most 64 MiB of HBM per device.

```python
import math
import jax
import jax.numpy as jnp
from jax import lax

NY = 1024
DEPTHS = 4
SWEEPS = 3
REGIONS = 4
NX = 256
FREQS = 32
SLICES = 32


def draw_slice_owner(key, part):
    middle = 1 + jax.random.permutation(jax.random.fold_in(key, 21), SLICES - 2)[:DEPTHS - 2]
    chosen = jnp.concatenate([jnp.array([0, SLICES - 1], dtype=jnp.int32), middle.astype(jnp.int32)])
    order = jax.random.permutation(jax.random.fold_in(key, 22), DEPTHS)
    return chosen[order].astype(jnp.int32)


def draw_region_map(key, part):
    edges = (jax.random.randint(jax.random.fold_in(key, 11), (NX, NY), 0, 8) == 0).astype(jnp.int32)
    starts = jax.random.randint(jax.random.fold_in(key, 12), (NX, 1), 0, REGIONS)
    return ((jnp.cumsum(edges, axis=1) + starts) % REGIONS).astype(jnp.int32)


def level_of(key, dims, cuts, least, top_value):
    factor_of = 1.0
    for position, blocks in cuts:
        steps = jax.random.uniform(jax.random.fold_in(jax.random.fold_in(key, 6), position), (blocks,), jnp.float32, least / len(cuts), top_value / len(cuts))
        factor_of = factor_of * jnp.repeat(jnp.exp(steps), dims[position] // blocks).reshape((-1,) + (1,) * (len(dims) - 1 - position))
    return factor_of


def centred(key, dims, deviation, reach, pieces=(), kind=jnp.bfloat16):
    loudness = level_of(key, dims, pieces, -0.22, 0.18) if pieces else 1.0
    entries = jax.random.normal(key, dims, jnp.float32) * deviation * loudness
    return jnp.minimum(jnp.maximum(entries, -reach), reach).astype(kind)


def setup_inputs(seed: int = 0) -> dict:
    key_list = jax.random.split(jax.random.key(seed), 6)
    return {
        "source_field": centred(key_list[0], (2, FREQS, NX, NY), 1.0, 6.0, ((1, 32), (2, 16)), jnp.float32),
        "receiver_field": centred(key_list[1], (2, FREQS, NX, NY), 1.0, 6.0, ((1, 32), (2, 16)), jnp.float32),
        "velocity_store": jnp.clip(0.5 + 0.5 * jax.random.uniform(key_list[2], (SLICES, NX, NY), jnp.float32) ** level_of(key_list[2], (SLICES, NX, NY), ((0, 32), (1, 16)), -0.2, 0.2), 0.5, 1.0),
        "slice_owner": draw_slice_owner(jax.random.fold_in(key_list[5], 71), 0),
        "region_map": draw_region_map(jax.random.fold_in(key_list[5], 71), 0),
    }


DAMPING = 0.125
ROTATION = 0.125
STEP_DEPTH = 4.0
SMOOTHING = 0.25

def laplace(wave):
    padded = jnp.pad(wave, ((0, 0), (1, 1), (1, 1)))
    center = padded[:, 1:-1, 1:-1]
    beside_x = padded[:, 2:, 1:-1] + padded[:, :-2, 1:-1]
    beside_y = padded[:, 1:-1, 2:] + padded[:, 1:-1, :-2]
    return beside_x + beside_y - 4.0 * center

def sweep_once(wave, coeff):
    spread = laplace(wave)
    real_part = wave[0] + DAMPING * spread[0] - coeff * spread[1]
    imag_part = wave[1] + DAMPING * spread[1] + coeff * spread[0]
    return jnp.stack([real_part, imag_part])

def rotate(wave, cosines, sines):
    return jnp.stack([wave[0] * cosines - wave[1] * sines, wave[0] * sines + wave[1] * cosines])

def reference(source_field, receiver_field, velocity_store, slice_owner, region_map):
    speeds = jnp.take(velocity_store, slice_owner, axis=0)

    def per_frequency(image_sum, freq_index):
        omega_now = 1.0 + freq_index.astype(jnp.float32) / FREQS
        source_now = lax.dynamic_index_in_dim(source_field, freq_index, 1, keepdims=False)
        receiver_now = lax.dynamic_index_in_dim(receiver_field, freq_index, 1, keepdims=False)
        layers = []
        for depth_no in range(DEPTHS):
            speed_map = speeds[depth_no]
            angles = omega_now * STEP_DEPTH / speed_map
            cosines = jnp.cos(angles)
            sines = jnp.sin(angles)
            source_now = rotate(source_now, cosines, sines)
            receiver_now = rotate(receiver_now, cosines, -sines)
            coeff = ROTATION * speed_map / omega_now
            for sweep_no in range(SWEEPS):
                source_now = sweep_once(source_now, coeff)
                receiver_now = sweep_once(receiver_now, -coeff)
            layers.append(source_now[0] * receiver_now[0] + source_now[1] * receiver_now[1])
        return (image_sum + jnp.stack(layers), jnp.stack([source_now, receiver_now]))
    image_sum, finals = lax.scan(per_frequency, jnp.zeros((DEPTHS, NX, NY), jnp.float32), jnp.arange(FREQS, dtype=jnp.int32))
    wavefields = jnp.moveaxis(finals, 0, 2)
    image_sum = image_sum / math.sqrt(FREQS)
    labels = region_map.astype(jnp.float32) + 1.0
    label_pad = jnp.pad(labels, ((0, 0), (1, 1)))
    image_pad = jnp.pad(image_sum, ((0, 0), (0, 0), (1, 1)))
    next_same = (label_pad[:, 2:] == labels).astype(jnp.float32)
    prev_same = (label_pad[:, :-2] == labels).astype(jnp.float32)
    smoothed = image_sum + SMOOTHING * (next_same * (image_pad[..., 2:] - image_sum) + prev_same * (image_pad[..., :-2] - image_sum))
    return (wavefields, smoothed)
```

```python
import functools
import math

import jax
import jax.numpy as jnp
from jax import lax
from jax.experimental import pallas as pl
from jax.experimental.pallas import tpu as pltpu
from jax.sharding import PartitionSpec as P

MESH = pl.DeviceIdType.MESH
DEPTHS = 4
SWEEPS = 3
HALO = DEPTHS * SWEEPS
ROWS = 16
DAMPING = 0.125
ROTATION = 0.125
STEP_DEPTH = 4.0
SMOOTHING = 0.25


def remote(src, dst, send, recv, device):
    return pltpu.make_async_remote_copy(
        src_ref=src,
        dst_ref=dst,
        send_sem=send,
        recv_sem=recv,
        device_id=device,
        device_id_type=MESH,
    )


def sin_cos(theta):
    turns = jnp.floor(theta * (2.0 / math.pi) + 0.5)
    rest = theta - turns * 1.5703125
    rest = rest - turns * 4.837512969970703125e-4
    rest = rest - turns * 7.54978995489188216e-8
    sq = rest * rest
    sine = ((-1.9515295891e-4 * sq + 8.3321608736e-3) * sq - 1.6666654611e-1) * sq * rest + rest
    cosine = (
        ((2.443315711809948e-5 * sq - 1.388731625493765e-3) * sq + 4.166664568298827e-2) * sq * sq
        - 0.5 * sq
        + 1.0
    )
    odd = turns - 2.0 * jnp.floor(turns * 0.5)
    back = turns - 4.0 * jnp.floor(turns * 0.25) - odd
    sign = 1.0 - back
    sin_val = jnp.where(odd > 0.5, cosine, sine) * sign
    cos_val = jnp.where(odd > 0.5, -sine, cosine) * sign
    return sin_val, cos_val


def kernel(
    freqs, tiles,
    src, rcv, vel, own, reg,
    wave_out, img_out,
    raw, velraw, regbuf, ownbuf, buf_a, buf_b, vels, stage, recv, labs, weights, imgb, pack, parts, wave, img,
    local_sem, first_sem, field_sem, vhalo_sem, z_sem, x_sem, core_sem, image_sem,
):
    f = lax.axis_index("freq")
    t = lax.axis_index("tile")
    after = lax.rem(t + 1, tiles)
    before = lax.rem(t + tiles - 1, tiles)
    core = lax.rem(f, 2)
    row = f // 2
    xx = row // 4
    zz = lax.rem(row, 4)

    barrier = pltpu.get_barrier_semaphore()

    def signal(i, carry):
        pl.semaphore_signal(
            barrier, inc=1, device_id=(lax.rem(f + i, freqs), t), device_id_type=MESH
        )
        return carry

    for tile in (after, before):
        pl.semaphore_signal(barrier, inc=1, device_id=(f, tile), device_id_type=MESH)
    lax.fori_loop(1, freqs, signal, 0)

    loads = [
        pltpu.make_async_copy(vel, velraw, local_sem.at[0]),
        pltpu.make_async_copy(reg, regbuf, local_sem.at[1]),
        pltpu.make_async_copy(own, ownbuf, local_sem.at[2]),
        pltpu.make_async_copy(src, raw.at[pl.ds(0, 2)], local_sem.at[3]),
        pltpu.make_async_copy(rcv, raw.at[pl.ds(2, 2)], local_sem.at[4]),
    ]
    for copy in loads:
        copy.start()

    loads[0].wait()
    for half in range(2):
        for c in range(8):
            stage[pl.ds(128 * half + 8 * (c // 4) + c % 4, 8, stride=16), :] = velraw[
                8 * half : 8 * half + 8, 128 * c : 128 * c + 128
            ]
    loads[1].wait()
    own_labels = regbuf[...].astype(jnp.float32) + 1.0
    own_labels = jnp.concatenate([own_labels[4 * m : 4 * m + 4] for m in range(4)], axis=1)
    for j in range(32):
        stage[8 * j + 4 : 8 * j + 8, :] = own_labels
    mine = pl.ds(pl.multiple_of(8 * f, 8), 8)
    recv[mine, :] = stage[mine, :]
    loads[3].wait()
    loads[4].wait()
    for a in range(4):
        for half in range(2):
            for c in range(8):
                buf_a[a, pl.ds(8 * (16 + 8 * half) + c, 8, stride=8), :] = raw[
                    a, 8 * half : 8 * half + 8, 128 * c : 128 * c + 128
                ]
    loads[2].wait()

    pl.semaphore_wait(barrier, freqs + 1)

    def first_send(i, carry):
        d = lax.rem(f + i, freqs)
        remote(
            stage.at[pl.ds(pl.multiple_of(8 * d, 8), 8)],
            recv.at[mine],
            first_sem.at[0],
            first_sem.at[1],
            (d, t),
        ).start()
        return carry

    lax.fori_loop(1, freqs, first_send, 0)
    fields = []
    for a in range(4):
        for k, (lo, to, tile) in enumerate(((20, 4, after), (16, 32, before))):
            fields.append(
                remote(
                    buf_a.at[a, pl.ds(8 * lo, 8 * HALO)],
                    buf_a.at[a, pl.ds(8 * to, 8 * HALO)],
                    field_sem.at[0, 2 * a + k],
                    field_sem.at[1, 2 * a + k],
                    (f, tile),
                )
            )
    for copy in fields:
        copy.start()

    bulk = pl.ds(0, 8 * (freqs - 1))
    first_wait = remote(stage.at[bulk], recv.at[bulk], first_sem.at[0], first_sem.at[1], (f, after))
    first_wait.wait_recv()
    wanted = [jnp.full((8, 128), ownbuf[d], jnp.int32) for d in range(DEPTHS)]
    picked = [jnp.ones((8, 128), jnp.float32)] * DEPTHS
    for j in range(32):
        piece = recv[8 * j : 8 * j + 8, :]
        picked = [jnp.where(w == j, piece, p) for w, p in zip(wanted, picked)]
    for c in range(2):

        @pl.when(core == c)
        def _():
            for d in range(DEPTHS):
                vels[d, 16 + row, 4 * c : 4 * c + 4, :] = picked[d][0:4]

    lanes = pl.ds(pl.multiple_of(4 * core, 4), 4)

    def block(part, first, count):
        return vels.at[:, pl.ds(16 * part + first, count), lanes]

    z_peers = [((xx * 4 + lax.rem(zz + i, 4)) * 2 + core, t) for i in (1, 2, 3)]
    x_peers = [((lax.rem(xx + i, 4) * 4 + zz) * 2 + core, t) for i in (1, 2, 3)]
    core_peer = (row * 2 + 1 - core, t)

    def spread(part, first, count, sems, peers):
        piece = block(part, first, count)
        copies = [
            remote(piece, piece, sems.at[0, part, i], sems.at[1, part, i], peer)
            for i, peer in enumerate(peers)
        ]
        for copy in copies:
            copy.start()
        return copies

    vhalos = [
        remote(block(1, row, 1), block(0, row, 1), vhalo_sem.at[0, 0], vhalo_sem.at[1, 0], (f, after)),
        remote(block(1, row, 1), block(2, row, 1), vhalo_sem.at[0, 1], vhalo_sem.at[1, 1], (f, before)),
    ]
    for copy in vhalos:
        copy.start()
    z_own = spread(1, row, 1, z_sem, z_peers)

    lane = lax.broadcasted_iota(jnp.int32, (8, 128), 1)
    sub = lax.broadcasted_iota(jnp.int32, (8, 128), 0)
    first_lane, last_lane = lane == 0, lane == 127
    start_cell = first_lane & (sub == 0)
    end_cell = last_lane & (sub == 7)
    group = [(lane >= 32 * m) & (lane < 32 * m + 32) for m in range(4)]

    def shifted(ref, at, middle):
        up = jnp.where(first_lane, ref[pl.ds(at + 1, 8), :], middle)
        down = jnp.where(last_lane, ref[pl.ds(at - 1, 8), :], middle)
        return pltpu.roll(up, 127, 1), pltpu.roll(down, 1, 1)

    for i in range(4):
        cols = [recv[pl.ds(8 * q + 4 + i, 8, stride=32), :] for q in range(4)]
        for m in range(4):
            total = None
            for q in range(4):
                moved = cols[q] if q == m else pltpu.roll(cols[q], (32 * (q - m)) % 128, 1)
                total = moved if total is None else jnp.where(group[q], moved, total)
            labs[8 * (4 * m + i + 1) : 8 * (4 * m + i + 2), :] = total
    scale = SMOOTHING / math.sqrt(freqs)
    for r in range(ROWS):
        middle = labs[8 * (r + 1) : 8 * (r + 2), :]
        up, down = shifted(labs, 8 * (r + 1), middle)
        weights[0, 8 * r : 8 * r + 8, :] = jnp.where((up == middle) & ~end_cell, scale, 0.0)
        weights[1, 8 * r : 8 * r + 8, :] = jnp.where((down == middle) & ~start_cell, scale, 0.0)

    for copy in z_own:
        copy.wait_recv()
    x_own = spread(1, 4 * xx, 4, x_sem, x_peers)
    for copy in vhalos:
        copy.wait_recv()
    z_halo = [spread(part, row, 1, z_sem, z_peers) for part in (0, 2)]
    for copy in x_own:
        copy.wait_recv()
    c_own = spread(1, 0, 16, core_sem, [core_peer])
    for copy in z_halo[0] + z_halo[1]:
        copy.wait_recv()
    x_halo = [spread(part, 4 * xx, 4, x_sem, x_peers) for part in (0, 2)]
    for copy in x_halo[0] + x_halo[1]:
        copy.wait_recv()
    c_halo = [spread(part, 0, 16, core_sem, [core_peer]) for part in (0, 2)]
    for copy in c_own + c_halo[0] + c_halo[1]:
        copy.wait_recv()
    for copy in fields:
        copy.wait()

    omega = 1.0 + f.astype(jnp.float32) / freqs
    reach = omega * STEP_DEPTH
    turn = ROTATION / omega

    def close(ref):
        zero = jnp.zeros((8, 128), jnp.float32)
        for edge, at in ((0, 15), (tiles - 1, 32)):

            @pl.when(t == edge)
            def _():
                for a in range(4):
                    ref[a, 8 * at : 8 * at + 8, :] = zero

    def rotate(ref, d, i):
        at = pl.ds(pl.multiple_of(8 * i, 8), 8)
        sine, cosine = sin_cos(reach / vels[d, i])
        s0, s1, r0, r1 = (ref[a, at, :] for a in range(4))
        ref[0, at, :] = s0 * cosine - s1 * sine
        ref[1, at, :] = s0 * sine + s1 * cosine
        ref[2, at, :] = r0 * cosine + r1 * sine
        ref[3, at, :] = r1 * cosine - r0 * sine

    def sweep(old, new, d, i):
        base = pl.multiple_of(8 * i, 8)
        coeff = vels[d, i] * turn
        middles, spreads = [], []
        for a in range(4):
            ref = old.at[a]
            middle = ref[pl.ds(base, 8), :]
            up, down = shifted(ref, base, middle)
            beside_y = jnp.where(end_cell, 0.0, up) + jnp.where(start_cell, 0.0, down)
            beside_x = ref[pl.ds(base + 8, 8), :] + ref[pl.ds(base - 8, 8), :]
            middles.append(middle)
            spreads.append(beside_x + beside_y - 4.0 * middle)
        for k, sign in ((0, 1.0), (2, -1.0)):
            signed = coeff * sign
            new[k, pl.ds(base, 8), :] = (
                middles[k] + DAMPING * spreads[k] - signed * spreads[k + 1]
            )
            new[k + 1, pl.ds(base, 8), :] = (
                middles[k + 1] + DAMPING * spreads[k + 1] + signed * spreads[k]
            )

    def over_rows(low, high, width, body):
        steps = (high - low) // width

        def go(n, carry):
            for k in range(width):
                body(low + width * n + k)
            return carry

        lax.fori_loop(0, steps, go, 0)
        for i in range(low + steps * width, high):
            body(i)

    close(buf_a)
    now, later = buf_a, buf_b
    bulk_pack = pl.ds(0, 4 * (freqs - 1))
    for d in range(DEPTHS):
        low = 4 + SWEEPS * d
        over_rows(low, 48 - low, 4, functools.partial(rotate, now, d))
        for s in range(SWEEPS):
            low += 1
            over_rows(low, 48 - low, 8, functools.partial(sweep, now, later, d))
            close(later)
            now, later = later, now

        for r in range(ROWS):
            at = slice(8 * (16 + r), 8 * (17 + r))
            imgb[8 * (r + 1) : 8 * (r + 2), :] = (
                now[0, at, :] * now[2, at, :] + now[1, at, :] * now[3, at, :]
            )
        smooth = []
        for r in range(ROWS):
            middle = imgb[8 * (r + 1) : 8 * (r + 2), :]
            up, down = shifted(imgb, 8 * (r + 1), middle)
            nxt, prv = weights[0, 8 * r : 8 * r + 8, :], weights[1, 8 * r : 8 * r + 8, :]
            smooth.append(
                middle * (1.0 / math.sqrt(freqs))
                + nxt * (jnp.where(end_cell, 0.0, up) - middle)
                + prv * (jnp.where(start_cell, 0.0, down) - middle)
            )
        for q in range(4):
            for i in range(4):
                total = None
                for m in range(4):
                    line = smooth[4 * m + i]
                    moved = line if m == q else pltpu.roll(line, (32 * (m - q)) % 128, 1)
                    total = moved if total is None else jnp.where(group[m], moved, total)
                pack[d, pl.ds(4 * q + i, 8, stride=16), :] = total
        own_piece = pl.ds(pl.multiple_of(4 * f, 4), 4)
        parts[d, own_piece, :] = pack[d, own_piece, :]

        def image_send(i, carry):
            to = lax.rem(f + i, freqs)
            remote(
                pack.at[d, pl.ds(pl.multiple_of(4 * to, 4), 4)],
                parts.at[d, own_piece],
                image_sem.at[0, d],
                image_sem.at[1, d],
                (to, t),
            ).start()
            return carry

        lax.fori_loop(1, freqs, image_send, 0)

    for a in range(4):
        for half in range(2):
            for c in range(8):
                wave[a, 8 * half : 8 * half + 8, 128 * c : 128 * c + 128] = now[
                    a, pl.ds(8 * (16 + 8 * half) + c, 8, stride=8), :
                ]
    wave_copy = pltpu.make_async_copy(wave, wave_out, local_sem.at[0])
    wave_copy.start()

    first_wait.wait_send()
    for copy in vhalos + z_own + x_own + c_own:
        copy.wait_send()
    for group_of in (z_halo, x_halo, c_halo):
        for copy in group_of[0] + group_of[1]:
            copy.wait_send()

    for d in range(DEPTHS):
        done = remote(
            pack.at[d, bulk_pack], parts.at[d, bulk_pack], image_sem.at[0, d], image_sem.at[1, d], (f, after)
        )
        done.wait_recv()
        total = parts[d, 0:8, :]
        for j in range(1, 16):
            total = total + parts[d, 8 * j : 8 * j + 8, :]
        total = total[0:4] + total[4:8]
        for m in range(4):
            img[d, 4 * m : 4 * m + 4, :] = total[:, 32 * m : 32 * m + 32]
        done.wait_send()
    img_copy = pltpu.make_async_copy(img, img_out, local_sem.at[1])
    img_copy.start()
    wave_copy.wait()
    img_copy.wait()


def solution(mesh):
    freqs, tiles = mesh.shape["freq"], mesh.shape["tile"]

    def on_device(source_field, receiver_field, velocity_store, slice_owner, region_map):
        any_space = pl.BlockSpec(memory_space=pl.ANY)
        f32 = jnp.float32
        wave, image = pl.pallas_call(
            functools.partial(kernel, freqs, tiles),
            out_shape=[
                jax.ShapeDtypeStruct((4, 16, 1024), f32),
                jax.ShapeDtypeStruct((DEPTHS, 16, 32), f32),
            ],
            in_specs=[any_space] * 5,
            out_specs=[any_space] * 2,
            scratch_shapes=[
                pltpu.VMEM((4, 16, 1024), f32),
                pltpu.VMEM((16, 1024), f32),
                pltpu.VMEM((16, 32), jnp.int32),
                pltpu.SMEM((DEPTHS,), jnp.int32),
                pltpu.VMEM((4, 48 * 8, 128), f32),
                pltpu.VMEM((4, 48 * 8, 128), f32),
                pltpu.VMEM((DEPTHS, 48, 8, 128), f32),
                pltpu.VMEM((32 * 8, 128), f32),
                pltpu.VMEM((32 * 8, 128), f32),
                pltpu.VMEM((18 * 8, 128), f32),
                pltpu.VMEM((2, 16 * 8, 128), f32),
                pltpu.VMEM((18 * 8, 128), f32),
                pltpu.VMEM((DEPTHS, 32 * 4, 128), f32),
                pltpu.VMEM((DEPTHS, 32 * 4, 128), f32),
                pltpu.VMEM((4, 16, 1024), f32),
                pltpu.VMEM((DEPTHS, 16, 32), f32),
                pltpu.SemaphoreType.DMA((5,)),
                pltpu.SemaphoreType.DMA((2,)),
                pltpu.SemaphoreType.DMA((2, 8)),
                pltpu.SemaphoreType.DMA((2, 2)),
                pltpu.SemaphoreType.DMA((2, 3, 3)),
                pltpu.SemaphoreType.DMA((2, 3, 3)),
                pltpu.SemaphoreType.DMA((2, 3, 1)),
                pltpu.SemaphoreType.DMA((2, DEPTHS)),
            ],
            compiler_params=pltpu.CompilerParams(
                collective_id=0, has_side_effects=True, vmem_limit_bytes=60 * 1024 * 1024
            ),
        )(
            source_field[:, 0],
            receiver_field[:, 0],
            velocity_store[0],
            slice_owner,
            region_map,
        )
        return wave.reshape(2, 2, 1, 16, 1024), image

    in_specs = (
        P(None, "freq", "tile", None),
        P(None, "freq", "tile", None),
        P("freq", "tile", None),
        P(),
        P("tile", "freq"),
    )
    out_specs = (P(None, None, "freq", "tile", None), P(None, "tile", "freq"))
    return jax.shard_map(
        on_device, mesh=mesh, in_specs=in_specs, out_specs=out_specs, check_vma=False
    )
```

```python
import functools
import math

import jax
import jax.numpy as jnp
from jax import lax
from jax.experimental import pallas as pl
from jax.experimental.pallas import tpu as pltpu
from jax.sharding import PartitionSpec as P

MESH = pl.DeviceIdType.MESH
DEPTHS = 4
SWEEPS = 3
HALO = DEPTHS * SWEEPS
ROWS = 16
CHUNKS = ((0, 3), (3, 6), (6, 8), (8, 12))
DAMPING = 0.125
ROTATION = 0.125
STEP_DEPTH = 4.0
SMOOTHING = 0.25


def remote(src, dst, send, recv, device):
    return pltpu.make_async_remote_copy(
        src_ref=src,
        dst_ref=dst,
        send_sem=send,
        recv_sem=recv,
        device_id=device,
        device_id_type=MESH,
    )


def sin_cos(theta):
    turns = jnp.floor(theta * (2.0 / math.pi) + 0.5)
    rest = theta - turns * 1.5703125
    rest = rest - turns * 4.837512969970703125e-4
    rest = rest - turns * 7.54978995489188216e-8
    sq = rest * rest
    sine = ((-1.9515295891e-4 * sq + 8.3321608736e-3) * sq - 1.6666654611e-1) * sq * rest + rest
    cosine = (
        ((2.443315711809948e-5 * sq - 1.388731625493765e-3) * sq + 4.166664568298827e-2) * sq * sq
        - 0.5 * sq
        + 1.0
    )
    odd = turns - 2.0 * jnp.floor(turns * 0.5)
    back = turns - 4.0 * jnp.floor(turns * 0.25) - odd
    sign = 1.0 - back
    sin_val = jnp.where(odd > 0.5, cosine, sine) * sign
    cos_val = jnp.where(odd > 0.5, -sine, cosine) * sign
    return sin_val, cos_val


def kernel(
    freqs, tiles,
    src, rcv, vel, own, reg,
    wave_out, img_out,
    raw, velraw, regbuf, ownbuf, buf_a, buf_b, vels, stage, recv, labs, weights, imgb, pack, parts, wave, img,
    local_sem, first_sem, field_sem, vhalo_sem, z_sem, x_sem, core_sem, image_sem,
):
    f = lax.axis_index("freq")
    t = lax.axis_index("tile")
    after = lax.rem(t + 1, tiles)
    before = lax.rem(t + tiles - 1, tiles)
    core = lax.rem(f, 2)
    row = f // 2
    xx = row // 4
    zz = lax.rem(row, 4)

    barrier = pltpu.get_barrier_semaphore()

    def signal(i, carry):
        pl.semaphore_signal(
            barrier, inc=1, device_id=(lax.rem(f + i, freqs), t), device_id_type=MESH
        )
        return carry

    for tile in (after, before):
        pl.semaphore_signal(barrier, inc=1, device_id=(f, tile), device_id_type=MESH)
    lax.fori_loop(1, freqs, signal, 0)

    loads = [
        pltpu.make_async_copy(vel, velraw, local_sem.at[0]),
        pltpu.make_async_copy(reg, regbuf, local_sem.at[1]),
        pltpu.make_async_copy(own, ownbuf, local_sem.at[2]),
        pltpu.make_async_copy(src, raw.at[pl.ds(0, 2)], local_sem.at[3]),
        pltpu.make_async_copy(rcv, raw.at[pl.ds(2, 2)], local_sem.at[4]),
    ]
    for copy in loads:
        copy.start()

    loads[0].wait()
    for half in range(2):
        for c in range(8):
            stage[pl.ds(128 * half + 8 * (c // 4) + c % 4, 8, stride=16), :] = velraw[
                8 * half : 8 * half + 8, 128 * c : 128 * c + 128
            ]
    loads[1].wait()
    own_labels = regbuf[...].astype(jnp.float32) + 1.0
    own_labels = jnp.concatenate([own_labels[4 * m : 4 * m + 4] for m in range(4)], axis=1)
    for j in range(32):
        stage[8 * j + 4 : 8 * j + 8, :] = own_labels
    mine = pl.ds(pl.multiple_of(8 * f, 8), 8)
    recv[mine, :] = stage[mine, :]
    loads[3].wait()
    loads[4].wait()
    for a in range(4):
        for half in range(2):
            for c in range(8):
                buf_a[a, pl.ds(8 * (16 + 8 * half) + c, 8, stride=8), :] = raw[
                    a, 8 * half : 8 * half + 8, 128 * c : 128 * c + 128
                ]
    loads[2].wait()

    pl.semaphore_wait(barrier, freqs + 1)

    def first_send(i, carry):
        d = lax.rem(f + i, freqs)
        remote(
            stage.at[pl.ds(pl.multiple_of(8 * d, 8), 8)],
            recv.at[mine],
            first_sem.at[0],
            first_sem.at[1],
            (d, t),
        ).start()
        return carry

    lax.fori_loop(1, freqs, first_send, 0)
    fields = []

    def send_fields(chunk):
        near, far = CHUNKS[chunk]
        count = 8 * (far - near)
        for a in range(4):
            for k, (lo, to, tile) in enumerate(
                ((32 - far, 16 - far, after), (16 + near, 32 + near, before))
            ):
                copy = remote(
                    buf_a.at[a, pl.ds(8 * lo, count)],
                    buf_a.at[a, pl.ds(8 * to, count)],
                    field_sem.at[0, chunk, 2 * a + k],
                    field_sem.at[1, chunk, 2 * a + k],
                    (f, tile),
                )
                copy.start()
                fields.append(copy)

    send_fields(0)

    bulk = pl.ds(0, 8 * (freqs - 1))
    first_wait = remote(stage.at[bulk], recv.at[bulk], first_sem.at[0], first_sem.at[1], (f, after))
    first_wait.wait_recv()
    wanted = [jnp.full((8, 128), ownbuf[d], jnp.int32) for d in range(DEPTHS)]
    picked = [jnp.ones((8, 128), jnp.float32)] * DEPTHS
    for j in range(32):
        piece = recv[8 * j : 8 * j + 8, :]
        picked = [jnp.where(w == j, piece, p) for w, p in zip(wanted, picked)]
    for c in range(2):

        @pl.when(core == c)
        def _():
            for d in range(DEPTHS):
                vels[d, 16 + row, 4 * c : 4 * c + 4, :] = picked[d][0:4]

    lanes = pl.ds(pl.multiple_of(4 * core, 4), 4)

    def block(part, first, count):
        return vels.at[:, pl.ds(16 * part + first, count), lanes]

    z_peers = [((xx * 4 + lax.rem(zz + i, 4)) * 2 + core, t) for i in (1, 2, 3)]
    x_peers = [((lax.rem(xx + i, 4) * 4 + zz) * 2 + core, t) for i in (1, 2, 3)]
    core_peer = (row * 2 + 1 - core, t)

    def spread(part, first, count, sems, peers):
        piece = block(part, first, count)
        copies = [
            remote(piece, piece, sems.at[0, part, i], sems.at[1, part, i], peer)
            for i, peer in enumerate(peers)
        ]
        for copy in copies:
            copy.start()
        return copies

    vhalos = [
        remote(block(1, row, 1), block(0, row, 1), vhalo_sem.at[0, 0], vhalo_sem.at[1, 0], (f, after)),
        remote(block(1, row, 1), block(2, row, 1), vhalo_sem.at[0, 1], vhalo_sem.at[1, 1], (f, before)),
    ]
    for copy in vhalos:
        copy.start()
    z_own = spread(1, row, 1, z_sem, z_peers)
    send_fields(1)

    lane = lax.broadcasted_iota(jnp.int32, (8, 128), 1)
    sub = lax.broadcasted_iota(jnp.int32, (8, 128), 0)
    first_lane, last_lane = lane == 0, lane == 127
    start_cell = first_lane & (sub == 0)
    end_cell = last_lane & (sub == 7)
    group = [(lane >= 32 * m) & (lane < 32 * m + 32) for m in range(4)]

    def shifted(ref, at, middle):
        up = jnp.where(first_lane, ref[pl.ds(at + 1, 8), :], middle)
        down = jnp.where(last_lane, ref[pl.ds(at - 1, 8), :], middle)
        return pltpu.roll(up, 127, 1), pltpu.roll(down, 1, 1)

    for i in range(4):
        cols = [recv[pl.ds(8 * q + 4 + i, 8, stride=32), :] for q in range(4)]
        for m in range(4):
            total = None
            for q in range(4):
                moved = cols[q] if q == m else pltpu.roll(cols[q], (32 * (q - m)) % 128, 1)
                total = moved if total is None else jnp.where(group[q], moved, total)
            labs[8 * (4 * m + i + 1) : 8 * (4 * m + i + 2), :] = total
    scale = SMOOTHING / math.sqrt(freqs)
    for r in range(ROWS):
        middle = labs[8 * (r + 1) : 8 * (r + 2), :]
        up, down = shifted(labs, 8 * (r + 1), middle)
        weights[0, 8 * r : 8 * r + 8, :] = jnp.where((up == middle) & ~end_cell, scale, 0.0)
        weights[1, 8 * r : 8 * r + 8, :] = jnp.where((down == middle) & ~start_cell, scale, 0.0)

    for copy in z_own:
        copy.wait_recv()
    x_own = spread(1, 4 * xx, 4, x_sem, x_peers)
    for copy in vhalos:
        copy.wait_recv()
    z_halo = [spread(part, row, 1, z_sem, z_peers) for part in (0, 2)]
    send_fields(2)
    for copy in x_own:
        copy.wait_recv()
    c_own = spread(1, 0, 16, core_sem, [core_peer])
    for copy in z_halo[0] + z_halo[1]:
        copy.wait_recv()
    x_halo = [spread(part, 4 * xx, 4, x_sem, x_peers) for part in (0, 2)]
    send_fields(3)
    for copy in x_halo[0] + x_halo[1]:
        copy.wait_recv()
    c_halo = [spread(part, 0, 16, core_sem, [core_peer]) for part in (0, 2)]
    for copy in c_own + c_halo[0] + c_halo[1]:
        copy.wait_recv()
    for copy in fields:
        copy.wait()

    omega = 1.0 + f.astype(jnp.float32) / freqs
    reach = omega * STEP_DEPTH
    turn = ROTATION / omega

    def close(ref):
        zero = jnp.zeros((8, 128), jnp.float32)
        for edge, at in ((0, 15), (tiles - 1, 32)):

            @pl.when(t == edge)
            def _():
                for a in range(4):
                    ref[a, 8 * at : 8 * at + 8, :] = zero

    def rotate(ref, d, i):
        at = pl.ds(pl.multiple_of(8 * i, 8), 8)
        sine, cosine = sin_cos(reach / vels[d, i])
        s0, s1, r0, r1 = (ref[a, at, :] for a in range(4))
        ref[0, at, :] = s0 * cosine - s1 * sine
        ref[1, at, :] = s0 * sine + s1 * cosine
        ref[2, at, :] = r0 * cosine + r1 * sine
        ref[3, at, :] = r1 * cosine - r0 * sine

    def sweep(old, new, d, i):
        base = pl.multiple_of(8 * i, 8)
        coeff = vels[d, i] * turn
        middles, spreads = [], []
        for a in range(4):
            ref = old.at[a]
            middle = ref[pl.ds(base, 8), :]
            up, down = shifted(ref, base, middle)
            beside_y = jnp.where(end_cell, 0.0, up) + jnp.where(start_cell, 0.0, down)
            beside_x = ref[pl.ds(base + 8, 8), :] + ref[pl.ds(base - 8, 8), :]
            middles.append(middle)
            spreads.append(beside_x + beside_y - 4.0 * middle)
        for k, sign in ((0, 1.0), (2, -1.0)):
            signed = coeff * sign
            new[k, pl.ds(base, 8), :] = (
                middles[k] + DAMPING * spreads[k] - signed * spreads[k + 1]
            )
            new[k + 1, pl.ds(base, 8), :] = (
                middles[k + 1] + DAMPING * spreads[k + 1] + signed * spreads[k]
            )

    def over_rows(low, high, width, body):
        steps = (high - low) // width

        def go(n, carry):
            for k in range(width):
                body(low + width * n + k)
            return carry

        lax.fori_loop(0, steps, go, 0)
        for i in range(low + steps * width, high):
            body(i)

    close(buf_a)
    now, later = buf_a, buf_b
    bulk_pack = pl.ds(0, 4 * (freqs - 1))
    for d in range(DEPTHS):
        low = 4 + SWEEPS * d
        over_rows(low, 48 - low, (48 - 2 * low) // 2, functools.partial(rotate, now, d))
        for s in range(SWEEPS):
            low += 1
            over_rows(low, 48 - low, (48 - 2 * low) // 2, functools.partial(sweep, now, later, d))
            close(later)
            now, later = later, now

        for r in range(ROWS):
            at = slice(8 * (16 + r), 8 * (17 + r))
            imgb[8 * (r + 1) : 8 * (r + 2), :] = (
                now[0, at, :] * now[2, at, :] + now[1, at, :] * now[3, at, :]
            )
        smooth = []
        for r in range(ROWS):
            middle = imgb[8 * (r + 1) : 8 * (r + 2), :]
            up, down = shifted(imgb, 8 * (r + 1), middle)
            nxt, prv = weights[0, 8 * r : 8 * r + 8, :], weights[1, 8 * r : 8 * r + 8, :]
            smooth.append(
                middle * (1.0 / math.sqrt(freqs))
                + nxt * (jnp.where(end_cell, 0.0, up) - middle)
                + prv * (jnp.where(start_cell, 0.0, down) - middle)
            )
        for q in range(4):
            for i in range(4):
                total = None
                for m in range(4):
                    line = smooth[4 * m + i]
                    moved = line if m == q else pltpu.roll(line, (32 * (m - q)) % 128, 1)
                    total = moved if total is None else jnp.where(group[m], moved, total)
                pack[d, pl.ds(4 * q + i, 8, stride=16), :] = total
        own_piece = pl.ds(pl.multiple_of(4 * f, 4), 4)
        parts[d, own_piece, :] = pack[d, own_piece, :]

        def image_send(i, carry):
            to = lax.rem(f + i, freqs)
            remote(
                pack.at[d, pl.ds(pl.multiple_of(4 * to, 4), 4)],
                parts.at[d, own_piece],
                image_sem.at[0, d],
                image_sem.at[1, d],
                (to, t),
            ).start()
            return carry

        lax.fori_loop(1, freqs, image_send, 0)

    for a in range(4):
        for half in range(2):
            for c in range(8):
                wave[a, 8 * half : 8 * half + 8, 128 * c : 128 * c + 128] = now[
                    a, pl.ds(8 * (16 + 8 * half) + c, 8, stride=8), :
                ]
    wave_copy = pltpu.make_async_copy(wave, wave_out, local_sem.at[0])
    wave_copy.start()

    first_wait.wait_send()
    for copy in vhalos + z_own + x_own + c_own:
        copy.wait_send()
    for group_of in (z_halo, x_halo, c_halo):
        for copy in group_of[0] + group_of[1]:
            copy.wait_send()

    for d in range(DEPTHS):
        done = remote(
            pack.at[d, bulk_pack], parts.at[d, bulk_pack], image_sem.at[0, d], image_sem.at[1, d], (f, after)
        )
        done.wait_recv()
        total = parts[d, 0:8, :]
        for j in range(1, 16):
            total = total + parts[d, 8 * j : 8 * j + 8, :]
        total = total[0:4] + total[4:8]
        for m in range(4):
            img[d, 4 * m : 4 * m + 4, :] = total[:, 32 * m : 32 * m + 32]
        done.wait_send()
    img_copy = pltpu.make_async_copy(img, img_out, local_sem.at[1])
    img_copy.start()
    wave_copy.wait()
    img_copy.wait()


def solution(mesh):
    freqs, tiles = mesh.shape["freq"], mesh.shape["tile"]

    def on_device(source_field, receiver_field, velocity_store, slice_owner, region_map):
        any_space = pl.BlockSpec(memory_space=pl.ANY)
        f32 = jnp.float32
        wave, image = pl.pallas_call(
            functools.partial(kernel, freqs, tiles),
            out_shape=[
                jax.ShapeDtypeStruct((4, 16, 1024), f32),
                jax.ShapeDtypeStruct((DEPTHS, 16, 32), f32),
            ],
            in_specs=[any_space] * 5,
            out_specs=[any_space] * 2,
            scratch_shapes=[
                pltpu.VMEM((4, 16, 1024), f32),
                pltpu.VMEM((16, 1024), f32),
                pltpu.VMEM((16, 32), jnp.int32),
                pltpu.SMEM((DEPTHS,), jnp.int32),
                pltpu.VMEM((4, 48 * 8, 128), f32),
                pltpu.VMEM((4, 48 * 8, 128), f32),
                pltpu.VMEM((DEPTHS, 48, 8, 128), f32),
                pltpu.VMEM((32 * 8, 128), f32),
                pltpu.VMEM((32 * 8, 128), f32),
                pltpu.VMEM((18 * 8, 128), f32),
                pltpu.VMEM((2, 16 * 8, 128), f32),
                pltpu.VMEM((18 * 8, 128), f32),
                pltpu.VMEM((DEPTHS, 32 * 4, 128), f32),
                pltpu.VMEM((DEPTHS, 32 * 4, 128), f32),
                pltpu.VMEM((4, 16, 1024), f32),
                pltpu.VMEM((DEPTHS, 16, 32), f32),
                pltpu.SemaphoreType.DMA((5,)),
                pltpu.SemaphoreType.DMA((2,)),
                pltpu.SemaphoreType.DMA((2, len(CHUNKS), 8)),
                pltpu.SemaphoreType.DMA((2, 2)),
                pltpu.SemaphoreType.DMA((2, 3, 3)),
                pltpu.SemaphoreType.DMA((2, 3, 3)),
                pltpu.SemaphoreType.DMA((2, 3, 1)),
                pltpu.SemaphoreType.DMA((2, DEPTHS)),
            ],
            compiler_params=pltpu.CompilerParams(
                collective_id=0, has_side_effects=True, vmem_limit_bytes=60 * 1024 * 1024
            ),
        )(
            source_field[:, 0],
            receiver_field[:, 0],
            velocity_store[0],
            slice_owner,
            region_map,
        )
        return wave.reshape(2, 2, 1, 16, 1024), image

    in_specs = (
        P(None, "freq", "tile", None),
        P(None, "freq", "tile", None),
        P("freq", "tile", None),
        P(),
        P("tile", "freq"),
    )
    out_specs = (P(None, None, "freq", "tile", None), P(None, "tile", "freq"))
    return jax.shard_map(
        on_device, mesh=mesh, in_specs=in_specs, out_specs=out_specs, check_vma=False
    )
```

```python
import functools
import math

import jax
import jax.numpy as jnp
from jax import lax
from jax.experimental import pallas as pl
from jax.experimental.pallas import tpu as pltpu
from jax.sharding import PartitionSpec as P

MESH = pl.DeviceIdType.MESH
DEPTHS = 4
SWEEPS = 3
HALO = DEPTHS * SWEEPS
ROWS = 16
CHUNKS = ((0, 3), (3, 6), (6, 7), (7, 12))
DAMPING = 0.125
ROTATION = 0.125
STEP_DEPTH = 4.0
SMOOTHING = 0.25


def remote(src, dst, send, recv, device):
    return pltpu.make_async_remote_copy(
        src_ref=src,
        dst_ref=dst,
        send_sem=send,
        recv_sem=recv,
        device_id=device,
        device_id_type=MESH,
    )


def sin_cos(theta):
    turns = jnp.floor(theta * (2.0 / math.pi) + 0.5)
    rest = theta - turns * 1.5703125
    rest = rest - turns * 4.837512969970703125e-4
    rest = rest - turns * 7.54978995489188216e-8
    sq = rest * rest
    sine = ((-1.9515295891e-4 * sq + 8.3321608736e-3) * sq - 1.6666654611e-1) * sq * rest + rest
    cosine = (
        ((2.443315711809948e-5 * sq - 1.388731625493765e-3) * sq + 4.166664568298827e-2) * sq * sq
        - 0.5 * sq
        + 1.0
    )
    odd = turns - 2.0 * jnp.floor(turns * 0.5)
    back = turns - 4.0 * jnp.floor(turns * 0.25) - odd
    sign = 1.0 - back
    sin_val = jnp.where(odd > 0.5, cosine, sine) * sign
    cos_val = jnp.where(odd > 0.5, -sine, cosine) * sign
    return sin_val, cos_val


def kernel(
    freqs, tiles,
    src, rcv, vel, own, reg,
    wave, img,
    raw, velraw, regbuf, ownbuf, buf_a, buf_b, vels, stage, recv, labs, weights, imgb, pack, parts,
    local_sem, first_sem, field_sem, vhalo_sem, z_sem, x_sem, core_sem, image_sem,
):
    f = lax.axis_index("freq")
    t = lax.axis_index("tile")
    after = lax.rem(t + 1, tiles)
    before = lax.rem(t + tiles - 1, tiles)
    core = lax.rem(f, 2)
    row = f // 2
    xx = row // 4
    zz = lax.rem(row, 4)

    loads = [
        pltpu.make_async_copy(vel, velraw, local_sem.at[0]),
        pltpu.make_async_copy(reg, regbuf, local_sem.at[1]),
        pltpu.make_async_copy(own, ownbuf, local_sem.at[2]),
        pltpu.make_async_copy(src, raw.at[pl.ds(0, 2)], local_sem.at[3]),
        pltpu.make_async_copy(rcv, raw.at[pl.ds(2, 2)], local_sem.at[4]),
    ]
    for copy in loads:
        copy.start()

    barrier = pltpu.get_barrier_semaphore()

    def signal(i, carry):
        pl.semaphore_signal(
            barrier, inc=1, device_id=(lax.rem(f + i, freqs), t), device_id_type=MESH
        )
        return carry

    for tile in (after, before):
        pl.semaphore_signal(barrier, inc=1, device_id=(f, tile), device_id_type=MESH)
    lax.fori_loop(1, freqs, signal, 0)

    loads[0].wait()
    for half in range(2):
        for c in range(8):
            stage[pl.ds(128 * half + 8 * (c // 4) + c % 4, 8, stride=16), :] = velraw[
                8 * half : 8 * half + 8, 128 * c : 128 * c + 128
            ]
    loads[1].wait()
    own_labels = regbuf[...].astype(jnp.float32) + 1.0
    own_labels = jnp.concatenate([own_labels[4 * m : 4 * m + 4] for m in range(4)], axis=1)
    for j in range(32):
        stage[8 * j + 4 : 8 * j + 8, :] = own_labels
    mine = pl.ds(pl.multiple_of(8 * f, 8), 8)
    recv[mine, :] = stage[mine, :]
    loads[3].wait()
    loads[4].wait()
    for a in range(4):
        for half in range(2):
            for c in range(8):
                buf_a[a, pl.ds(8 * (16 + 8 * half) + c, 8, stride=8), :] = raw[
                    a, 8 * half : 8 * half + 8, 128 * c : 128 * c + 128
                ]
    loads[2].wait()

    pl.semaphore_wait(barrier, freqs + 1)

    def first_send(i, carry):
        d = lax.rem(f + i, freqs)
        remote(
            stage.at[pl.ds(pl.multiple_of(8 * d, 8), 8)],
            recv.at[mine],
            first_sem.at[0],
            first_sem.at[1],
            (d, t),
        ).start()
        return carry

    lax.fori_loop(1, freqs, first_send, 0)
    fields = []

    def send_fields(chunk):
        near, far = CHUNKS[chunk]
        count = 8 * (far - near)
        for a in range(4):
            for k, (lo, to, tile) in enumerate(
                ((32 - far, 16 - far, after), (16 + near, 32 + near, before))
            ):
                copy = remote(
                    buf_a.at[a, pl.ds(8 * lo, count)],
                    buf_a.at[a, pl.ds(8 * to, count)],
                    field_sem.at[0, chunk, 2 * a + k],
                    field_sem.at[1, chunk, 2 * a + k],
                    (f, tile),
                )
                copy.start()
                fields.append(copy)

    send_fields(0)

    bulk = pl.ds(0, 8 * (freqs - 1))
    first_wait = remote(stage.at[bulk], recv.at[bulk], first_sem.at[0], first_sem.at[1], (f, after))
    first_wait.wait_recv()
    wanted = [jnp.full((8, 128), ownbuf[d], jnp.int32) for d in range(DEPTHS)]
    picked = [jnp.ones((8, 128), jnp.float32)] * DEPTHS
    for j in range(32):
        piece = recv[8 * j : 8 * j + 8, :]
        picked = [jnp.where(w == j, piece, p) for w, p in zip(wanted, picked)]
    for c in range(2):

        @pl.when(core == c)
        def _():
            for d in range(DEPTHS):
                vels[d, 16 + row, 4 * c : 4 * c + 4, :] = picked[d][0:4]

    lanes = pl.ds(pl.multiple_of(4 * core, 4), 4)

    def block(part, first, count):
        return vels.at[:, pl.ds(16 * part + first, count), lanes]

    z_peers = [((xx * 4 + lax.rem(zz + i, 4)) * 2 + core, t) for i in (1, 2, 3)]
    x_peers = [((lax.rem(xx + i, 4) * 4 + zz) * 2 + core, t) for i in (1, 2, 3)]
    core_peer = (row * 2 + 1 - core, t)

    def spread(part, first, count, sems, peers):
        piece = block(part, first, count)
        copies = [
            remote(piece, piece, sems.at[0, part, i], sems.at[1, part, i], peer)
            for i, peer in enumerate(peers)
        ]
        for copy in copies:
            copy.start()
        return copies

    vhalos = [
        remote(block(1, row, 1), block(0, row, 1), vhalo_sem.at[0, 0], vhalo_sem.at[1, 0], (f, after)),
        remote(block(1, row, 1), block(2, row, 1), vhalo_sem.at[0, 1], vhalo_sem.at[1, 1], (f, before)),
    ]
    for copy in vhalos:
        copy.start()
    z_own = spread(1, row, 1, z_sem, z_peers)
    send_fields(1)

    lane = lax.broadcasted_iota(jnp.int32, (8, 128), 1)
    sub = lax.broadcasted_iota(jnp.int32, (8, 128), 0)
    first_lane, last_lane = lane == 0, lane == 127
    start_cell = first_lane & (sub == 0)
    end_cell = last_lane & (sub == 7)
    group = [(lane >= 32 * m) & (lane < 32 * m + 32) for m in range(4)]

    def shifted(ref, at, middle):
        up = jnp.where(first_lane, ref[pl.ds(at + 1, 8), :], middle)
        down = jnp.where(last_lane, ref[pl.ds(at - 1, 8), :], middle)
        return pltpu.roll(up, 127, 1), pltpu.roll(down, 1, 1)

    for i in range(4):
        cols = [recv[pl.ds(8 * q + 4 + i, 8, stride=32), :] for q in range(4)]
        for m in range(4):
            total = None
            for q in range(4):
                moved = cols[q] if q == m else pltpu.roll(cols[q], (32 * (q - m)) % 128, 1)
                total = moved if total is None else jnp.where(group[q], moved, total)
            labs[8 * (4 * m + i + 1) : 8 * (4 * m + i + 2), :] = total
    scale = SMOOTHING / math.sqrt(freqs)
    for r in range(ROWS):
        middle = labs[8 * (r + 1) : 8 * (r + 2), :]
        up, down = shifted(labs, 8 * (r + 1), middle)
        weights[0, 8 * r : 8 * r + 8, :] = jnp.where((up == middle) & ~end_cell, scale, 0.0)
        weights[1, 8 * r : 8 * r + 8, :] = jnp.where((down == middle) & ~start_cell, scale, 0.0)

    for copy in z_own:
        copy.wait_recv()
    x_own = spread(1, 4 * xx, 4, x_sem, x_peers)
    for copy in vhalos:
        copy.wait_recv()
    z_halo = [spread(part, row, 1, z_sem, z_peers) for part in (0, 2)]
    send_fields(2)
    for copy in x_own:
        copy.wait_recv()
    c_own = spread(1, 0, 16, core_sem, [core_peer])
    for copy in z_halo[0] + z_halo[1]:
        copy.wait_recv()
    x_halo = [spread(part, 4 * xx, 4, x_sem, x_peers) for part in (0, 2)]
    send_fields(3)
    for copy in x_halo[0] + x_halo[1]:
        copy.wait_recv()
    c_halo = [spread(part, 0, 16, core_sem, [core_peer]) for part in (0, 2)]
    for copy in c_own + c_halo[0] + c_halo[1]:
        copy.wait_recv()
    for copy in fields:
        copy.wait()

    omega = 1.0 + f.astype(jnp.float32) / freqs
    reach = omega * STEP_DEPTH
    turn = ROTATION / omega

    def close(ref):
        zero = jnp.zeros((8, 128), jnp.float32)
        for edge, at in ((0, 15), (tiles - 1, 32)):

            @pl.when(t == edge)
            def _():
                for a in range(4):
                    ref[a, 8 * at : 8 * at + 8, :] = zero

    def rotate(ref, d, i):
        at = pl.ds(pl.multiple_of(8 * i, 8), 8)
        sine, cosine = sin_cos(reach / vels[d, i])
        s0, s1, r0, r1 = (ref[a, at, :] for a in range(4))
        ref[0, at, :] = s0 * cosine - s1 * sine
        ref[1, at, :] = s0 * sine + s1 * cosine
        ref[2, at, :] = r0 * cosine + r1 * sine
        ref[3, at, :] = r1 * cosine - r0 * sine

    def sweep(old, new, d, i):
        base = pl.multiple_of(8 * i, 8)
        coeff = vels[d, i] * turn
        middles, spreads = [], []
        for a in range(4):
            ref = old.at[a]
            middle = ref[pl.ds(base, 8), :]
            up, down = shifted(ref, base, middle)
            beside_y = jnp.where(end_cell, 0.0, up) + jnp.where(start_cell, 0.0, down)
            beside_x = ref[pl.ds(base + 8, 8), :] + ref[pl.ds(base - 8, 8), :]
            middles.append(middle)
            spreads.append(beside_x + beside_y - 4.0 * middle)
        for k, sign in ((0, 1.0), (2, -1.0)):
            signed = coeff * sign
            new[k, pl.ds(base, 8), :] = (
                middles[k] + DAMPING * spreads[k] - signed * spreads[k + 1]
            )
            new[k + 1, pl.ds(base, 8), :] = (
                middles[k + 1] + DAMPING * spreads[k + 1] + signed * spreads[k]
            )

    def over_rows(low, high, width, body):
        steps = (high - low) // width

        def go(n, carry):
            for k in range(width):
                body(low + width * n + k)
            return carry

        lax.fori_loop(0, steps, go, 0)
        for i in range(low + steps * width, high):
            body(i)

    close(buf_a)
    now, later = buf_a, buf_b
    bulk_pack = pl.ds(0, 4 * (freqs - 1))
    for d in range(DEPTHS):
        low = 4 + SWEEPS * d
        over_rows(low, 48 - low, (48 - 2 * low) // 2, functools.partial(rotate, now, d))
        for s in range(SWEEPS):
            low += 1
            over_rows(low, 48 - low, 48 - 2 * low, functools.partial(sweep, now, later, d))
            close(later)
            now, later = later, now

        for r in range(ROWS):
            at = slice(8 * (16 + r), 8 * (17 + r))
            imgb[8 * (r + 1) : 8 * (r + 2), :] = (
                now[0, at, :] * now[2, at, :] + now[1, at, :] * now[3, at, :]
            )
        smooth = []
        for r in range(ROWS):
            middle = imgb[8 * (r + 1) : 8 * (r + 2), :]
            up, down = shifted(imgb, 8 * (r + 1), middle)
            nxt, prv = weights[0, 8 * r : 8 * r + 8, :], weights[1, 8 * r : 8 * r + 8, :]
            smooth.append(
                middle * (1.0 / math.sqrt(freqs))
                + nxt * (jnp.where(end_cell, 0.0, up) - middle)
                + prv * (jnp.where(start_cell, 0.0, down) - middle)
            )
        for q in range(4):
            for i in range(4):
                total = None
                for m in range(4):
                    line = smooth[4 * m + i]
                    moved = line if m == q else pltpu.roll(line, (32 * (m - q)) % 128, 1)
                    total = moved if total is None else jnp.where(group[m], moved, total)
                pack[d, pl.ds(4 * q + i, 8, stride=16), :] = total
        own_piece = pl.ds(pl.multiple_of(4 * f, 4), 4)
        parts[d, own_piece, :] = pack[d, own_piece, :]

        def image_send(i, carry):
            to = lax.rem(f + i, freqs)
            remote(
                pack.at[d, pl.ds(pl.multiple_of(4 * to, 4), 4)],
                parts.at[d, own_piece],
                image_sem.at[0, d],
                image_sem.at[1, d],
                (to, t),
            ).start()
            return carry

        lax.fori_loop(1, freqs, image_send, 0)

    for a in range(4):
        for half in range(2):
            for c in range(8):
                wave[a, 8 * half : 8 * half + 8, 128 * c : 128 * c + 128] = now[
                    a, pl.ds(8 * (16 + 8 * half) + c, 8, stride=8), :
                ]

    first_wait.wait_send()
    for copy in vhalos + z_own + x_own + c_own:
        copy.wait_send()
    for group_of in (z_halo, x_halo, c_halo):
        for copy in group_of[0] + group_of[1]:
            copy.wait_send()

    for d in range(DEPTHS):
        done = remote(
            pack.at[d, bulk_pack], parts.at[d, bulk_pack], image_sem.at[0, d], image_sem.at[1, d], (f, after)
        )
        done.wait_recv()
        total = parts[d, 0:8, :]
        for j in range(1, 16):
            total = total + parts[d, 8 * j : 8 * j + 8, :]
        total = total[0:4] + total[4:8]
        for m in range(4):
            img[d, 4 * m : 4 * m + 4, :] = total[:, 32 * m : 32 * m + 32]
        done.wait_send()


def solution(mesh):
    freqs, tiles = mesh.shape["freq"], mesh.shape["tile"]

    def on_device(source_field, receiver_field, velocity_store, slice_owner, region_map):
        any_space = pl.BlockSpec(memory_space=pl.ANY)
        f32 = jnp.float32
        wave, image = pl.pallas_call(
            functools.partial(kernel, freqs, tiles),
            out_shape=[
                pltpu.VMEM((4, 16, 1024), f32),
                pltpu.VMEM((DEPTHS, 16, 32), f32),
            ],
            in_specs=[any_space] * 5,
            out_specs=[pl.BlockSpec(memory_space=pltpu.VMEM)] * 2,
            scratch_shapes=[
                pltpu.VMEM((4, 16, 1024), f32),
                pltpu.VMEM((16, 1024), f32),
                pltpu.VMEM((16, 32), jnp.int32),
                pltpu.SMEM((DEPTHS,), jnp.int32),
                pltpu.VMEM((4, 48 * 8, 128), f32),
                pltpu.VMEM((4, 48 * 8, 128), f32),
                pltpu.VMEM((DEPTHS, 48, 8, 128), f32),
                pltpu.VMEM((32 * 8, 128), f32),
                pltpu.VMEM((32 * 8, 128), f32),
                pltpu.VMEM((18 * 8, 128), f32),
                pltpu.VMEM((2, 16 * 8, 128), f32),
                pltpu.VMEM((18 * 8, 128), f32),
                pltpu.VMEM((DEPTHS, 32 * 4, 128), f32),
                pltpu.VMEM((DEPTHS, 32 * 4, 128), f32),
                pltpu.SemaphoreType.DMA((5,)),
                pltpu.SemaphoreType.DMA((2,)),
                pltpu.SemaphoreType.DMA((2, len(CHUNKS), 8)),
                pltpu.SemaphoreType.DMA((2, 2)),
                pltpu.SemaphoreType.DMA((2, 3, 3)),
                pltpu.SemaphoreType.DMA((2, 3, 3)),
                pltpu.SemaphoreType.DMA((2, 3, 1)),
                pltpu.SemaphoreType.DMA((2, DEPTHS)),
            ],
            compiler_params=pltpu.CompilerParams(
                collective_id=0, has_side_effects=True, vmem_limit_bytes=60 * 1024 * 1024
            ),
        )(
            source_field[:, 0],
            receiver_field[:, 0],
            velocity_store[0],
            slice_owner,
            region_map,
        )
        return wave.reshape(2, 2, 1, 16, 1024), image

    in_specs = (
        P(None, "freq", "tile", None),
        P(None, "freq", "tile", None),
        P("freq", "tile", None),
        P(),
        P("tile", "freq"),
    )
    out_specs = (P(None, None, "freq", "tile", None), P(None, "tile", "freq"))
    return jax.shard_map(
        on_device, mesh=mesh, in_specs=in_specs, out_specs=out_specs, check_vma=False
    )
```

```python
import functools
import math

import jax
import jax.numpy as jnp
from jax import lax
from jax.experimental import pallas as pl
from jax.experimental.pallas import tpu as pltpu
from jax.sharding import PartitionSpec as P

MESH = pl.DeviceIdType.MESH
DEPTHS = 4
SWEEPS = 3
HALO = DEPTHS * SWEEPS
ROWS = 16
CHUNKS = ((0, 3), (3, 6), (6, 7), (7, 12))
DAMPING = 0.125
ROTATION = 0.125
STEP_DEPTH = 4.0
SMOOTHING = 0.25


def remote(src, dst, send, recv, device):
    return pltpu.make_async_remote_copy(
        src_ref=src,
        dst_ref=dst,
        send_sem=send,
        recv_sem=recv,
        device_id=device,
        device_id_type=MESH,
    )


def sin_cos(theta):
    turns = jnp.floor(theta * (2.0 / math.pi) + 0.5)
    rest = theta - turns * 1.5703125
    rest = rest - turns * 4.837512969970703125e-4
    rest = rest - turns * 7.54978995489188216e-8
    sq = rest * rest
    sine = ((-1.9515295891e-4 * sq + 8.3321608736e-3) * sq - 1.6666654611e-1) * sq * rest + rest
    cosine = (
        ((2.443315711809948e-5 * sq - 1.388731625493765e-3) * sq + 4.166664568298827e-2) * sq * sq
        - 0.5 * sq
        + 1.0
    )
    odd = turns - 2.0 * jnp.floor(turns * 0.5)
    back = turns - 4.0 * jnp.floor(turns * 0.25) - odd
    sign = 1.0 - back
    sin_val = jnp.where(odd > 0.5, cosine, sine) * sign
    cos_val = jnp.where(odd > 0.5, -sine, cosine) * sign
    return sin_val, cos_val


def kernel(
    freqs, tiles,
    src, rcv, vel, own, reg,
    wave, img,
    raw, velraw, regbuf, ownbuf, buf_a, buf_b, vels, stage, recv, label_in, labs, weights, imgb, pack, parts,
    local_sem, first_sem, label_sem, field_sem, vhalo_sem, z_sem, x_sem, core_sem, image_sem,
):
    f = lax.axis_index("freq")
    t = lax.axis_index("tile")
    after = lax.rem(t + 1, tiles)
    before = lax.rem(t + tiles - 1, tiles)
    core = lax.rem(f, 2)
    row = f // 2
    xx = row // 4
    zz = lax.rem(row, 4)

    loads = [
        pltpu.make_async_copy(vel, velraw, local_sem.at[0]),
        pltpu.make_async_copy(reg, regbuf, local_sem.at[1]),
        pltpu.make_async_copy(own, ownbuf, local_sem.at[2]),
        pltpu.make_async_copy(src, raw.at[pl.ds(0, 2)], local_sem.at[3]),
        pltpu.make_async_copy(rcv, raw.at[pl.ds(2, 2)], local_sem.at[4]),
    ]
    for copy in loads:
        copy.start()

    barrier = pltpu.get_barrier_semaphore()

    def signal(i, carry):
        pl.semaphore_signal(
            barrier, inc=1, device_id=(lax.rem(f + i, freqs), t), device_id_type=MESH
        )
        return carry

    for tile in (after, before):
        pl.semaphore_signal(barrier, inc=1, device_id=(f, tile), device_id_type=MESH)
    lax.fori_loop(1, freqs, signal, 0)

    loads[0].wait()
    for half in range(2):
        for c in range(8):
            stage[pl.ds(128 * half + 8 * (c // 4) + c % 4, 8, stride=16), :] = velraw[
                8 * half : 8 * half + 8, 128 * c : 128 * c + 128
            ]
    loads[1].wait()
    own_labels = regbuf[...].astype(jnp.float32) + 1.0
    own_labels = jnp.concatenate([own_labels[4 * m : 4 * m + 4] for m in range(4)], axis=1)
    held = pl.ds(pl.multiple_of(4 * (16 * core + row), 4), 4)
    label_in[held, :] = own_labels
    mine = pl.ds(pl.multiple_of(8 * f, 8), 4)
    recv[mine, :] = stage[mine, :]
    loads[3].wait()
    loads[4].wait()
    for a in range(4):
        for half in range(2):
            for c in range(8):
                buf_a[a, pl.ds(8 * (16 + 8 * half) + c, 8, stride=8), :] = raw[
                    a, 8 * half : 8 * half + 8, 128 * c : 128 * c + 128
                ]
    loads[2].wait()

    pl.semaphore_wait(barrier, freqs + 1)

    def first_send(i, carry):
        d = lax.rem(f + i, freqs)
        remote(
            stage.at[pl.ds(pl.multiple_of(8 * d, 8), 4)],
            recv.at[mine],
            first_sem.at[0],
            first_sem.at[1],
            (d, t),
        ).start()
        return carry

    lax.fori_loop(1, freqs, first_send, 0)
    fields = []

    def send_fields(chunk):
        near, far = CHUNKS[chunk]
        count = 8 * (far - near)
        for a in range(4):
            for k, (lo, to, tile) in enumerate(
                ((32 - far, 16 - far, after), (16 + near, 32 + near, before))
            ):
                copy = remote(
                    buf_a.at[a, pl.ds(8 * lo, count)],
                    buf_a.at[a, pl.ds(8 * to, count)],
                    field_sem.at[0, chunk, 2 * a + k],
                    field_sem.at[1, chunk, 2 * a + k],
                    (f, tile),
                )
                copy.start()
                fields.append(copy)

    send_fields(0)

    bulk = pl.ds(0, 4 * (freqs - 1))
    first_wait = remote(stage.at[bulk], recv.at[bulk], first_sem.at[0], first_sem.at[1], (f, after))
    first_wait.wait_recv()
    wanted = [jnp.full((8, 128), ownbuf[d], jnp.int32) for d in range(DEPTHS)]
    picked = [jnp.ones((8, 128), jnp.float32)] * DEPTHS
    for j in range(32):
        piece = recv[8 * j : 8 * j + 8, :]
        picked = [jnp.where(w == j, piece, p) for w, p in zip(wanted, picked)]
    for c in range(2):

        @pl.when(core == c)
        def _():
            for d in range(DEPTHS):
                vels[d, 16 + row, 4 * c : 4 * c + 4, :] = picked[d][0:4]

    lanes = pl.ds(pl.multiple_of(4 * core, 4), 4)

    def block(part, first, count):
        return vels.at[:, pl.ds(16 * part + first, count), lanes]

    z_peers = [((xx * 4 + lax.rem(zz + i, 4)) * 2 + core, t) for i in (1, 2, 3)]
    x_peers = [((lax.rem(xx + i, 4) * 4 + zz) * 2 + core, t) for i in (1, 2, 3)]
    core_peer = (row * 2 + 1 - core, t)

    def spread(part, first, count, sems, peers):
        piece = block(part, first, count)
        copies = [
            remote(piece, piece, sems.at[0, part, i], sems.at[1, part, i], peer)
            for i, peer in enumerate(peers)
        ]
        for copy in copies:
            copy.start()
        return copies

    vhalos = [
        remote(block(1, row, 1), block(0, row, 1), vhalo_sem.at[0, 0], vhalo_sem.at[1, 0], (f, after)),
        remote(block(1, row, 1), block(2, row, 1), vhalo_sem.at[0, 1], vhalo_sem.at[1, 1], (f, before)),
    ]
    for copy in vhalos:
        copy.start()
    z_own = spread(1, row, 1, z_sem, z_peers)

    def share(first, count, stage_no, peers):
        piece = label_in.at[pl.ds(pl.multiple_of(4 * (16 * core + first), 4), 4 * count)]
        copies = [
            remote(piece, piece, label_sem.at[0, stage_no, i], label_sem.at[1, stage_no, i], peer)
            for i, peer in enumerate(peers)
        ]
        for copy in copies:
            copy.start()
        return copies

    label_z = share(row, 1, 0, z_peers)
    send_fields(1)

    lane = lax.broadcasted_iota(jnp.int32, (8, 128), 1)
    sub = lax.broadcasted_iota(jnp.int32, (8, 128), 0)
    first_lane, last_lane = lane == 0, lane == 127
    start_cell = first_lane & (sub == 0)
    end_cell = last_lane & (sub == 7)
    group = [(lane >= 32 * m) & (lane < 32 * m + 32) for m in range(4)]

    def shifted(ref, at, middle):
        up = jnp.where(first_lane, ref[pl.ds(at + 1, 8), :], middle)
        down = jnp.where(last_lane, ref[pl.ds(at - 1, 8), :], middle)
        return pltpu.roll(up, 127, 1), pltpu.roll(down, 1, 1)

    for copy in z_own:
        copy.wait_recv()
    x_own = spread(1, 4 * xx, 4, x_sem, x_peers)
    for copy in vhalos:
        copy.wait_recv()
    z_halo = [spread(part, row, 1, z_sem, z_peers) for part in (0, 2)]
    send_fields(2)
    for copy in label_z:
        copy.wait_recv()
    label_x = share(4 * xx, 4, 1, x_peers)
    for copy in x_own:
        copy.wait_recv()
    c_own = spread(1, 0, 16, core_sem, [core_peer])
    for copy in z_halo[0] + z_halo[1]:
        copy.wait_recv()
    x_halo = [spread(part, 4 * xx, 4, x_sem, x_peers) for part in (0, 2)]
    send_fields(3)
    for copy in label_x:
        copy.wait_recv()
    label_c = share(0, 16, 2, [core_peer])
    for copy in x_halo[0] + x_halo[1]:
        copy.wait_recv()
    c_halo = [spread(part, 0, 16, core_sem, [core_peer]) for part in (0, 2)]
    for copy in c_own + c_halo[0] + c_halo[1] + label_c:
        copy.wait_recv()
    for i in range(4):
        cols = [label_in[pl.ds(64 * (q % 2) + 4 * (q // 2) + i, 8, stride=8), :] for q in range(4)]
        for m in range(4):
            total = None
            for q in range(4):
                moved = cols[q] if q == m else pltpu.roll(cols[q], (32 * (q - m)) % 128, 1)
                total = moved if total is None else jnp.where(group[q], moved, total)
            labs[8 * (4 * m + i + 1) : 8 * (4 * m + i + 2), :] = total
    scale = SMOOTHING / math.sqrt(freqs)
    for r in range(ROWS):
        middle = labs[8 * (r + 1) : 8 * (r + 2), :]
        up, down = shifted(labs, 8 * (r + 1), middle)
        weights[0, 8 * r : 8 * r + 8, :] = jnp.where((up == middle) & ~end_cell, scale, 0.0)
        weights[1, 8 * r : 8 * r + 8, :] = jnp.where((down == middle) & ~start_cell, scale, 0.0)

    for copy in fields:
        copy.wait()

    omega = 1.0 + f.astype(jnp.float32) / freqs
    reach = omega * STEP_DEPTH
    turn = ROTATION / omega

    def close(ref):
        zero = jnp.zeros((8, 128), jnp.float32)
        for edge, at in ((0, 15), (tiles - 1, 32)):

            @pl.when(t == edge)
            def _():
                for a in range(4):
                    ref[a, 8 * at : 8 * at + 8, :] = zero

    def rotate(ref, d, i):
        at = pl.ds(pl.multiple_of(8 * i, 8), 8)
        sine, cosine = sin_cos(reach / vels[d, i])
        s0, s1, r0, r1 = (ref[a, at, :] for a in range(4))
        ref[0, at, :] = s0 * cosine - s1 * sine
        ref[1, at, :] = s0 * sine + s1 * cosine
        ref[2, at, :] = r0 * cosine + r1 * sine
        ref[3, at, :] = r1 * cosine - r0 * sine

    def sweep(old, new, d, i):
        base = pl.multiple_of(8 * i, 8)
        coeff = vels[d, i] * turn
        middles, spreads = [], []
        for a in range(4):
            ref = old.at[a]
            middle = ref[pl.ds(base, 8), :]
            up, down = shifted(ref, base, middle)
            beside_y = jnp.where(end_cell, 0.0, up) + jnp.where(start_cell, 0.0, down)
            beside_x = ref[pl.ds(base + 8, 8), :] + ref[pl.ds(base - 8, 8), :]
            middles.append(middle)
            spreads.append(beside_x + beside_y - 4.0 * middle)
        for k, sign in ((0, 1.0), (2, -1.0)):
            signed = coeff * sign
            new[k, pl.ds(base, 8), :] = (
                middles[k] + DAMPING * spreads[k] - signed * spreads[k + 1]
            )
            new[k + 1, pl.ds(base, 8), :] = (
                middles[k + 1] + DAMPING * spreads[k + 1] + signed * spreads[k]
            )

    def over_rows(low, high, width, body):
        steps = (high - low) // width

        def go(n, carry):
            for k in range(width):
                body(low + width * n + k)
            return carry

        lax.fori_loop(0, steps, go, 0)
        for i in range(low + steps * width, high):
            body(i)

    close(buf_a)
    now, later = buf_a, buf_b
    bulk_pack = pl.ds(0, 4 * (freqs - 1))
    for d in range(DEPTHS):
        low = 4 + SWEEPS * d
        over_rows(low, 48 - low, (48 - 2 * low) // 2, functools.partial(rotate, now, d))
        for s in range(SWEEPS):
            low += 1
            over_rows(low, 48 - low, 48 - 2 * low, functools.partial(sweep, now, later, d))
            close(later)
            now, later = later, now

        for r in range(ROWS):
            at = slice(8 * (16 + r), 8 * (17 + r))
            imgb[8 * (r + 1) : 8 * (r + 2), :] = (
                now[0, at, :] * now[2, at, :] + now[1, at, :] * now[3, at, :]
            )
        smooth = []
        for r in range(ROWS):
            middle = imgb[8 * (r + 1) : 8 * (r + 2), :]
            up, down = shifted(imgb, 8 * (r + 1), middle)
            nxt, prv = weights[0, 8 * r : 8 * r + 8, :], weights[1, 8 * r : 8 * r + 8, :]
            smooth.append(
                middle * (1.0 / math.sqrt(freqs))
                + nxt * (jnp.where(end_cell, 0.0, up) - middle)
                + prv * (jnp.where(start_cell, 0.0, down) - middle)
            )
        for q in range(4):
            for i in range(4):
                total = None
                for m in range(4):
                    line = smooth[4 * m + i]
                    moved = line if m == q else pltpu.roll(line, (32 * (m - q)) % 128, 1)
                    total = moved if total is None else jnp.where(group[m], moved, total)
                pack[d, pl.ds(4 * q + i, 8, stride=16), :] = total
        own_piece = pl.ds(pl.multiple_of(4 * f, 4), 4)
        parts[d, own_piece, :] = pack[d, own_piece, :]

        def image_send(i, carry):
            to = lax.rem(f + i, freqs)
            remote(
                pack.at[d, pl.ds(pl.multiple_of(4 * to, 4), 4)],
                parts.at[d, own_piece],
                image_sem.at[0, d],
                image_sem.at[1, d],
                (to, t),
            ).start()
            return carry

        lax.fori_loop(1, freqs, image_send, 0)

    for a in range(4):
        for half in range(2):
            for c in range(8):
                wave[a, 8 * half : 8 * half + 8, 128 * c : 128 * c + 128] = now[
                    a, pl.ds(8 * (16 + 8 * half) + c, 8, stride=8), :
                ]

    first_wait.wait_send()
    for copy in vhalos + z_own + x_own + c_own + label_z + label_x + label_c:
        copy.wait_send()
    for group_of in (z_halo, x_halo, c_halo):
        for copy in group_of[0] + group_of[1]:
            copy.wait_send()

    for d in range(DEPTHS):
        done = remote(
            pack.at[d, bulk_pack], parts.at[d, bulk_pack], image_sem.at[0, d], image_sem.at[1, d], (f, after)
        )
        done.wait_recv()
        total = parts[d, 0:8, :]
        for j in range(1, 16):
            total = total + parts[d, 8 * j : 8 * j + 8, :]
        total = total[0:4] + total[4:8]
        for m in range(4):
            img[d, 4 * m : 4 * m + 4, :] = total[:, 32 * m : 32 * m + 32]
        done.wait_send()


def solution(mesh):
    freqs, tiles = mesh.shape["freq"], mesh.shape["tile"]

    def on_device(source_field, receiver_field, velocity_store, slice_owner, region_map):
        any_space = pl.BlockSpec(memory_space=pl.ANY)
        f32 = jnp.float32
        wave, image = pl.pallas_call(
            functools.partial(kernel, freqs, tiles),
            out_shape=[
                pltpu.VMEM((4, 16, 1024), f32),
                pltpu.VMEM((DEPTHS, 16, 32), f32),
            ],
            in_specs=[any_space] * 5,
            out_specs=[pl.BlockSpec(memory_space=pltpu.VMEM)] * 2,
            scratch_shapes=[
                pltpu.VMEM((4, 16, 1024), f32),
                pltpu.VMEM((16, 1024), f32),
                pltpu.VMEM((16, 32), jnp.int32),
                pltpu.SMEM((DEPTHS,), jnp.int32),
                pltpu.VMEM((4, 48 * 8, 128), f32),
                pltpu.VMEM((4, 48 * 8, 128), f32),
                pltpu.VMEM((DEPTHS, 48, 8, 128), f32),
                pltpu.VMEM((32 * 8, 128), f32),
                pltpu.VMEM((32 * 8, 128), f32),
                pltpu.VMEM((32 * 4, 128), f32),
                pltpu.VMEM((18 * 8, 128), f32),
                pltpu.VMEM((2, 16 * 8, 128), f32),
                pltpu.VMEM((18 * 8, 128), f32),
                pltpu.VMEM((DEPTHS, 32 * 4, 128), f32),
                pltpu.VMEM((DEPTHS, 32 * 4, 128), f32),
                pltpu.SemaphoreType.DMA((5,)),
                pltpu.SemaphoreType.DMA((2,)),
                pltpu.SemaphoreType.DMA((2, 3, 3)),
                pltpu.SemaphoreType.DMA((2, len(CHUNKS), 8)),
                pltpu.SemaphoreType.DMA((2, 2)),
                pltpu.SemaphoreType.DMA((2, 3, 3)),
                pltpu.SemaphoreType.DMA((2, 3, 3)),
                pltpu.SemaphoreType.DMA((2, 3, 1)),
                pltpu.SemaphoreType.DMA((2, DEPTHS)),
            ],
            compiler_params=pltpu.CompilerParams(
                collective_id=0, has_side_effects=True, vmem_limit_bytes=60 * 1024 * 1024
            ),
        )(
            source_field[:, 0],
            receiver_field[:, 0],
            velocity_store[0],
            slice_owner,
            region_map,
        )
        return wave.reshape(2, 2, 1, 16, 1024), image

    in_specs = (
        P(None, "freq", "tile", None),
        P(None, "freq", "tile", None),
        P("freq", "tile", None),
        P(),
        P("tile", "freq"),
    )
    out_specs = (P(None, None, "freq", "tile", None), P(None, "tile", "freq"))
    return jax.shard_map(
        on_device, mesh=mesh, in_specs=in_specs, out_specs=out_specs, check_vma=False
    )
```
